32 devices in a mesh: rows: 16 (over z, x, core), cols: 2 (over y).
Axes of the slice: x: 2, y: 2, z: 4, core: 2. Of those that a mesh axis runs over, the one named last changes fastest.
Arguments:
- right_side: float32 [4, 2, 4096, 512], P(None, 'cols', 'rows'), may hold values from -6 to 6
- inverse_blocks: bfloat16 [4, 2, 4096, 8192], P(None, None, 'rows', 'cols'), may hold values from -0.09375 to 0.09375
- lower_blocks: bfloat16 [6, 2, 4096, 8192], P(None, None, 'rows', 'cols'), may hold values from -0.046875 to 0.046875
Outputs:
- solution: float32 [4, 2, 4096, 512], P(None, 'cols', 'rows')
The draws below stay inside these ranges and needn't reach their ends.
All inputs are finite; a program needn't handle non-finite values.
Results may differ from the reference program's by a relative error of at most 0.014.
Values may be sent and summed in bfloat16 or wider, within the bound.
No kernel may reach another device: no remote copies, remote signals or barrier semaphores. Data moves between devices by JAX's collectives and lax.ppermute only.
A program may use at most 128 MiB of HBM per device.

```python
import jax
import jax.numpy as jnp

PANEL = 8192
NP = 4
NRHS = 512
SUB = 4096
PAIRS = 6
N_COLS = 2


def with_spikes(drawn, own_key, source, target, blocks, factor):
    owner, partner = [(jnp.arange(drawn.shape[axis_at]) // (drawn.shape[axis_at] // blocks)).reshape([-1 if axis == axis_at else 1 for axis in range(drawn.ndim)]) for axis_at in (source, target)]
    chosen = jax.random.permutation(own_key, blocks)[partner]
    strong = (owner == chosen) | (owner == (partner + blocks // 2) % blocks)
    return jnp.where(strong, factor * drawn, drawn)


def block_scale(own_key, dims, shards, least, top_value):
    def one(axis_at, blocks):
        draws = jax.random.uniform(jax.random.fold_in(jax.random.fold_in(own_key, 6), axis_at), (blocks,), jnp.float32, least / len(shards), top_value / len(shards))
        return jnp.repeat(jnp.exp(draws), dims[axis_at] // blocks).reshape((-1,) + (1,) * (len(dims) - axis_at - 1))

    level = one(*shards[0])
    for cut in shards[1:]:
        level = level * one(*cut)
    return level


def bell_draw(stream_key, shape, spread, bound, cuts=(), dtype=jnp.bfloat16):
    result = jax.random.normal(stream_key, shape, jnp.float32) * spread
    if len(cuts) > 0:
        result = block_scale(stream_key, shape, cuts, -0.22, 0.18) * result
    return jnp.clip(result, min=-bound, max=bound).astype(dtype)


def heavy_noise(own_key, dims, width, reach, cuts, heavy, held_as=jnp.bfloat16):
    result = width * jax.random.normal(own_key, dims, jnp.float32)
    if cuts:
        result = result * block_scale(own_key, dims, cuts, -0.22, 0.18)
    return jnp.clip(with_spikes(result, jax.random.fold_in(own_key, 3), *heavy), -reach, reach).astype(held_as)


def setup_inputs(seed: int = 0) -> dict:
    key_list = jax.random.split(jax.random.key(seed), 4)
    return {
        "right_side": bell_draw(key_list[0], (NP, N_COLS, SUB, NRHS), 1.0, 6.0, ((1, 2), (2, 16)), jnp.float32),
        "inverse_blocks": heavy_noise(key_list[1], (NP, N_COLS, SUB, PANEL), PANEL ** -0.5, 0.09375, ((2, 16), (3, 2)), (3, 1, 2, 2.0)),
        "lower_blocks": heavy_noise(key_list[2], (PAIRS, N_COLS, SUB, PANEL), (PANEL * NP) ** -0.5, 0.046875, ((2, 16), (3, 2)), (3, 1, 2, 2.0)),
    }


def pair_index(target, source):
    return target * (target - 1) // 2 + source


def reference(right_side, inverse_blocks, lower_blocks):
    solved_list = []
    rounded_list = []
    for current in range(NP):
        running = jnp.zeros((PANEL, NRHS), jnp.float32)
        for source in range(current):
            factor_block = lower_blocks[pair_index(current, source)].reshape(PANEL, PANEL)
            running = running + jnp.dot(factor_block, rounded_list[source], preferred_element_type=jnp.float32)
        residual = (right_side[current].reshape(PANEL, NRHS) - running).astype(jnp.bfloat16)
        inverse_block = inverse_blocks[current].reshape(PANEL, PANEL)
        solved = jnp.dot(inverse_block, residual, preferred_element_type=jnp.float32)
        solved_list.append(solved.reshape(N_COLS, SUB, NRHS))
        rounded_list.append(solved.astype(jnp.bfloat16))
    return jnp.stack(solved_list)
```

```python
import functools

import jax
import jax.numpy as jnp
from jax import lax
from jax.experimental import pallas as pl
from jax.experimental.pallas import tpu as pltpu
from jax.sharding import PartitionSpec as P


def pair_index(target, source):
    return target * (target - 1) // 2 + source


def swap(block, mask, rows):
    return lax.ppermute(block, "rows", [(i, i ^ mask) for i in range(rows)])


def gather_rows(block, rows):
    height = block.shape[0]
    half = height // 2
    if rows != 16:
        everything = lax.all_gather(block, "rows", axis=0, tiled=True)
        return [(everything, None)]
    join = lambda *parts: jnp.concatenate(parts, axis=0)
    far = swap(block, 8, rows)
    near = swap(block, 4, rows)
    side = swap(block, 2, rows)
    by_near = swap(join(far, side[:half]), 4, rows)
    by_side = swap(join(far, near[half:]), 2, rows)
    last_side = swap(by_near[:half], 2, rows)
    last_near = swap(by_side[half:height], 4, rows)
    stages = [
        (join(block, far, near, side), [(0, 0, height), (8, 0, height), (4, 0, height), (2, 0, height)]),
        (join(by_near, by_side), [(12, 0, height), (6, 0, half), (10, 0, height), (6, half, half)]),
        (join(last_side, last_near), [(14, 0, half), (14, half, half)]),
    ]
    pieces = []
    for array, parts in stages:
        pieces.append((array, parts))
        pieces.append((swap(array, 1, rows), [(mask + 1, start, count) for mask, start, count in parts]))
    return pieces


def product_kernel(parts, has_total, where_ref, factor_ref, *refs):
    piece_refs = refs[: len(parts)]
    total_ref = refs[len(parts)] if has_total else None
    out_refs = refs[len(parts) + has_total : -1]
    vector_ref = refs[-1]
    own_row, own_group = where_ref[0], where_ref[1]
    groups, height, _ = factor_ref.shape
    for piece_ref, inside in zip(piece_refs, parts, strict=True):
        if inside is None:
            vector_ref[...] = piece_ref[...]
            continue
        offset = 0
        for mask, start, count in inside:
            place = pl.multiple_of((own_row ^ mask) * height + start, count)
            vector_ref[pl.ds(place, count)] = piece_ref[offset : offset + count]
            offset += count
    vector = vector_ref[...]
    for turn in range(groups):
        group = lax.rem(own_group + 1 + turn, groups)
        result = jnp.dot(factor_ref[group], vector, preferred_element_type=jnp.float32)
        span = pl.ds(turn * height, height)
        if has_total:
            result = result + total_ref[span]
        if len(out_refs) == 1:
            out_refs[0][span] = result
        elif turn < groups - 1:
            out_refs[0][span] = result.astype(jnp.bfloat16)
        else:
            out_refs[1][...] = result


def product(where, factor, pieces, total, split):
    groups, height, width = factor.shape
    columns = pieces[0][0].shape[1]
    full = groups * height
    if split:
        out_shape = (
            jax.ShapeDtypeStruct((full - height, columns), jnp.bfloat16),
            jax.ShapeDtypeStruct((height, columns), jnp.float32),
        )
    else:
        out_shape = (jax.ShapeDtypeStruct((full, columns), jnp.float32),)
    vmem = pl.BlockSpec(memory_space=pltpu.VMEM)
    operands = [where, factor, *(array for array, _ in pieces)] + ([] if total is None else [total])
    return pl.pallas_call(
        functools.partial(product_kernel, [parts for _, parts in pieces], total is not None),
        out_shape=out_shape,
        in_specs=[pl.BlockSpec(memory_space=pltpu.SMEM)] + [vmem] * (len(operands) - 1),
        out_specs=tuple(vmem for _ in out_shape),
        scratch_shapes=[pltpu.VMEM((width, columns), jnp.bfloat16)],
        compiler_params=pltpu.CompilerParams(vmem_limit_bytes=20 * 1024 * 1024),
        cost_estimate=pl.CostEstimate(
            flops=2 * full * width * columns,
            bytes_accessed=2 * (full * width + width * columns) + 4 * full * columns,
            transcendentals=0,
        ),
    )(*operands)


def fold_cols(sends, keep, cols):
    height = keep.shape[0]
    total = keep
    for step in range(1, cols):
        share = sends[(step - 1) * height : step * height]
        came = lax.ppermute(share, "cols", [(i, (i + step) % cols) for i in range(cols)])
        total = total + came.astype(jnp.float32)
    return total


def forward_solve(rows, cols, right_side, inverse_blocks, lower_blocks):
    panels, _, height, columns = right_side.shape
    where = jnp.stack([lax.axis_index("rows"), lax.axis_index("cols")]).astype(jnp.int32)
    chunks = 2 if rows == 16 and cols == 2 else 1
    width = columns // chunks
    solved = [[None] * chunks for _ in range(panels)]
    totals = [{} for _ in range(chunks)]
    pieces = [None] * chunks
    for current in range(panels):
        inverse_blocks, lower_blocks, right_side = lax.optimization_barrier((inverse_blocks, lower_blocks, right_side))
        inverse = inverse_blocks[current]
        lowers = {later: lower_blocks[pair_index(later, current - 1)] for later in range(current, panels) if current > 0}
        for chunk in range(chunks):
            residual = right_side[current, 0, :, chunk * width : (chunk + 1) * width]
            if current > 0:
                factor = lowers[current]
                sends, keep = product(where, factor, pieces[chunk], totals[chunk].pop(current, None), True)
                residual = residual - fold_cols(sends, keep, cols)
                for later in range(current + 1, panels):
                    factor = lowers[later]
                    (totals[chunk][later],) = product(
                        where, factor, pieces[chunk], totals[chunk].get(later), False
                    )
            around = gather_rows(residual.astype(jnp.bfloat16), rows)
            sends, keep = product(where, inverse, around, None, True)
            answer = fold_cols(sends, keep, cols)
            solved[current][chunk] = answer
            if current + 1 < panels:
                pieces[chunk] = gather_rows(answer.astype(jnp.bfloat16), rows)
    return jnp.stack([jnp.concatenate(part, axis=1) for part in solved])[:, None]


def solution(mesh):
    return jax.shard_map(
        functools.partial(forward_solve, mesh.shape["rows"], mesh.shape["cols"]),
        mesh=mesh,
        in_specs=(
            P(None, "cols", "rows", None),
            P(None, None, "rows", "cols"),
            P(None, None, "rows", "cols"),
        ),
        out_specs=P(None, "cols", "rows", None),
        check_vma=False,
    )
```

```python
import functools

import jax
import jax.numpy as jnp
from jax import lax
from jax.experimental import pallas as pl
from jax.experimental.pallas import tpu as pltpu
from jax.sharding import PartitionSpec as P

VMEM = pl.BlockSpec(memory_space=pltpu.VMEM)
ANY = pl.BlockSpec(memory_space=pl.ANY)
MIB = 1024 * 1024


def pair_index(target, source):
    return target * (target - 1) // 2 + source


def swap(block, rows, even, odd=None):
    odd = even if odd is None else odd
    return lax.ppermute(block, "rows", [(i, i ^ (odd if i % 2 else even)) for i in range(rows)])


def local_call(kernel, out_shape, operands, after, limit, cost=None):
    return pl.pallas_call(
        kernel,
        out_shape=out_shape,
        in_specs=[VMEM] * len(operands) + [ANY] * len(after),
        out_specs=tuple(VMEM for _ in out_shape),
        compiler_params=pltpu.CompilerParams(vmem_limit_bytes=limit * MIB),
        cost_estimate=pl.CostEstimate(flops=cost or 0, bytes_accessed=1024, transcendentals=0),
    )(*operands, *after)


def pack_kernel(sources, layout, *refs):
    for out_ref, spans in zip(refs[len(refs) - len(layout) :], layout):
        at = 0
        for source, start, count in spans:
            out_ref[at : at + count] = refs[source][start : start + count]
            at += count


def pack(sources, layout, after):
    columns, dtype = sources[0].shape[1], sources[0].dtype
    shapes = tuple(jax.ShapeDtypeStruct((sum(span[2] for span in spans), columns), dtype) for spans in layout)
    return local_call(functools.partial(pack_kernel, len(sources), layout), shapes, sources, after, 6)


class Gather:
    def __init__(self, block, rows):
        self.block, self.rows = block, rows
        self.height = block.shape[0]
        self.half = self.height // 2
        self.pieces = []
        self.split = rows == 16
        if self.split:
            self.far, self.near, self.side = (swap(block, rows, mask) for mask in (8, 4, 2))
        else:
            self.pieces.append((lax.all_gather(block, "rows", axis=0, tiled=True), None))

    def add(self, array, parts):
        self.pieces.append((array, parts))
        self.pieces.append((swap(array, self.rows, 1), [(mask + 1, start, count) for mask, start, count in parts]))

    def second(self, after):
        height, half = self.height, self.half
        self.for_near, self.for_side = pack(
            [self.far, self.near, self.side],
            [[(0, 0, height), (2, 0, half)], [(0, 0, height), (1, half, half)]],
            after,
        )
        self.by_near = swap(self.for_near, self.rows, 4)
        self.by_side = swap(self.for_side, self.rows, 2)

    def joining(self):
        return [self.block, self.far, self.near, self.side, self.by_near, self.by_side] if self.split else []

    def third(self, joined, other):
        height, half = self.height, self.half
        self.add(
            joined,
            [(mask, 0, height) for mask in (0, 8, 4, 2)]
            + [(12, 0, height), (6, 0, half), (10, 0, height), (6, half, half)],
        )
        self.last = swap(other, self.rows, 2, 4)

    def fourth(self):
        height = self.height
        (self.tail,) = pack([self.last], [[(0, 0, height)]], [])
        self.add(self.tail, [(14, 0, height)])


def product_kernel(parts, has_total, factor_ref, *refs):
    own_row, own_group = lax.axis_index("rows"), lax.axis_index("cols")
    groups, height, _ = factor_ref.shape
    send_ref, keep_ref, vector_ref = refs[-3:]
    for piece_ref, spans in zip(refs, parts):
        if spans is None:
            vector_ref[...] = piece_ref[...]
            continue
        at = 0
        for mask, start, count in spans:
            place = pl.multiple_of((own_row ^ mask) * height + start, count)
            vector_ref[pl.ds(place, count)] = piece_ref[at : at + count]
            at += count
    vector = vector_ref[...]
    for turn in range(groups):
        group = lax.rem(own_group + 1 + turn, groups)
        span = pl.ds(turn * height, height)
        result = jnp.dot(factor_ref[group], vector, preferred_element_type=jnp.float32)
        if has_total:
            result = result + refs[len(parts)][span]
        if turn < groups - 1:
            send_ref[span] = result.astype(send_ref.dtype)
        else:
            keep_ref[...] = result


def total_kernel(has_total, factor_ref, vector_ref, *refs):
    own_group = lax.axis_index("cols")
    groups, height, _ = factor_ref.shape
    vector = vector_ref[...]
    for turn in range(groups):
        group = lax.rem(own_group + 1 + turn, groups)
        span = pl.ds(turn * height, height)
        result = jnp.dot(factor_ref[group], vector, preferred_element_type=jnp.float32)
        refs[-1][span] = result + refs[0][span] if has_total else result


def product(factor, pieces, total, after):
    groups, height, width = factor.shape
    columns = pieces[0][0].shape[1]
    given = [] if total is None else [total]
    return local_call(
        functools.partial(product_kernel, [spans for _, spans in pieces], len(given)),
        (
            jax.ShapeDtypeStruct(((groups - 1) * height, columns), jnp.bfloat16),
            jax.ShapeDtypeStruct((height, columns), jnp.float32),
            jax.ShapeDtypeStruct((width, columns), jnp.bfloat16),
        ),
        [factor, *(array for array, _ in pieces), *given],
        after,
        14,
    )


def add_product(factor, vector, total):
    groups, height, width = factor.shape
    columns = vector.shape[1]
    given = [] if total is None else [total]
    return local_call(
        functools.partial(total_kernel, len(given)),
        (jax.ShapeDtypeStruct((groups * height, columns), jnp.float32),),
        [factor, vector, *given],
        [],
        14,
        2 * groups * height * width * columns,
    )[0]


def fold_kernel(shares, has_right, joins, keep_ref, *refs):
    total = keep_ref[...]
    for share_ref in refs[:shares]:
        total = total + share_ref[...].astype(jnp.float32)
    outs = list(refs[shares + has_right + joins :])
    if has_right:
        outs.pop(0)[...] = (refs[shares][...] - total).astype(jnp.bfloat16)
    else:
        outs.pop(0)[...] = total.astype(jnp.bfloat16)
        outs.pop(0)[...] = total
    if joins:
        joined_ref, other_ref = outs
        sources = refs[shares + has_right :][:joins]
        at = 0
        for source_ref in sources:
            count = source_ref.shape[0]
            joined_ref[at : at + count] = source_ref[...]
            at += count
        is_odd = lax.rem(lax.axis_index("rows"), 2) == 1
        height = other_ref.shape[0]
        other_ref[...] = jnp.where(is_odd, sources[5][:height], sources[4][:height])


def fold(keep, shares, right, joining):
    rounded = jax.ShapeDtypeStruct(keep.shape, jnp.bfloat16)
    given = [] if right is None else [right]
    out_shape = [rounded]
    if right is None:
        out_shape.append(jax.ShapeDtypeStruct(keep.shape, jnp.float32))
    if joining:
        rows, columns = sum(array.shape[0] for array in joining), keep.shape[1]
        out_shape.append(jax.ShapeDtypeStruct((rows, columns), jnp.bfloat16))
        out_shape.append(jax.ShapeDtypeStruct(keep.shape, jnp.bfloat16))
    kernel = functools.partial(fold_kernel, len(shares), len(given), len(joining))
    return list(local_call(kernel, tuple(out_shape), [keep, *shares, *given, *joining], [], 8))


def start_third(joining):
    height = joining[0].shape[0]
    is_odd = lax.rem(lax.axis_index("rows"), 2) == 1
    (joined,) = pack(joining, [[(i, 0, array.shape[0]) for i, array in enumerate(joining)]], [])
    return joined, jnp.where(is_odd, joining[5][:height], joining[4][:height])


def forward_solve(rows, cols, right_side, inverse_blocks, lower_blocks):
    panels, _, height, columns = right_side.shape
    chunks = 2 if rows == 16 and cols == 2 else 1
    width = columns // chunks
    steps = 2 * panels - 1
    solved = [[None] * chunks for _ in range(panels)]
    totals = [{} for _ in range(chunks)]
    factors = {}

    def right(current, chunk):
        return right_side[current, 0, :, chunk * width : (chunk + 1) * width]

    def load(step, after):
        current = step // 2
        blocks = inverse_blocks if step % 2 == 0 else lower_blocks
        if after is not None:
            blocks, _ = lax.optimization_barrier((blocks, after))
        if step % 2 == 0:
            loaded = {current: blocks[current]}
        else:
            loaded = {later: blocks[pair_index(later, current)] for later in range(current + 1, panels)}
        factors[step] = loaded
        return list(loaded.values())

    def multiply(step, chunk, gather, after):
        current, solving = step // 2, step % 2 == 0
        first = current if solving else current + 1
        total = None if solving else totals[chunk].pop(first, None)
        sends, keep, vector = product(factors[step][first], gather.pieces, total, after)
        made = []
        if not solving:
            for later in range(current + 2, panels):
                old = totals[chunk].get(later)
                totals[chunk][later] = add_product(factors[step][later], vector, old)
                made.append(totals[chunk][later])
        return sends, keep, made

    def finish(step, chunk, sends, keep, following):
        current, solving = step // 2, step % 2 == 0
        shares = []
        for turn in range(1, cols):
            share = sends[(turn - 1) * height : turn * height]
            shares.append(lax.ppermute(share, "cols", [(i, (i + turn) % cols) for i in range(cols)]))
        joining = following.joining() if following else []
        made = fold(keep, shares, None if solving else right(current + 1, chunk), joining)
        vectors[chunk] = made.pop(0)
        if solving:
            solved[current][chunk] = made.pop(0)
        if joining:
            following.third(*made)

    vectors = [right(0, chunk).astype(jnp.bfloat16) for chunk in range(chunks)]
    load(0, None)
    if chunks == 1:
        for step in range(steps):
            if step + 1 < steps:
                load(step + 1, vectors[0])
            sends, keep, _ = multiply(step, 0, Gather(vectors[0], rows), [])
            finish(step, 0, sends, keep, None)
    else:
        made = []
        gather = Gather(vectors[0], rows)
        gather.second([])
        gather.third(*start_third(gather.joining()))
        for step in range(steps):
            for chunk in range(chunks):
                other = 1 - chunk
                following = None
                gather.fourth()
                if step + chunk < steps:
                    following = Gather(vectors[other], rows)
                    loaded = load(step + 1, vectors[other]) if chunk == 0 and step + 1 < steps else []
                    following.second([gather.tail, *made, *loaded])
                sends, keep, made = multiply(step, chunk, gather, [following.for_near] if following else [])
                finish(step, chunk, sends, keep, following)
                gather = following
    return jnp.stack([jnp.concatenate(part, axis=1) for part in solved])[:, None]


def solution(mesh):
    return jax.shard_map(
        functools.partial(forward_solve, mesh.shape["rows"], mesh.shape["cols"]),
        mesh=mesh,
        in_specs=(
            P(None, "cols", "rows", None),
            P(None, None, "rows", "cols"),
            P(None, None, "rows", "cols"),
        ),
        out_specs=P(None, "cols", "rows", None),
        check_vma=False,
    )
```

```python
import functools

import jax
import jax.numpy as jnp
from jax import lax
from jax.experimental import pallas as pl
from jax.experimental.pallas import tpu as pltpu
from jax.sharding import PartitionSpec as P

VMEM = pl.BlockSpec(memory_space=pltpu.VMEM)
ANY = pl.BlockSpec(memory_space=pl.ANY)
MIB = 1024 * 1024


def pair_index(target, source):
    return target * (target - 1) // 2 + source


def swap(block, rows, even, odd=None):
    odd = even if odd is None else odd
    return lax.ppermute(block, "rows", [(i, i ^ (odd if i % 2 else even)) for i in range(rows)])


def local_call(kernel, out_shape, operands, after, limit, cost=None):
    return pl.pallas_call(
        kernel,
        out_shape=out_shape,
        in_specs=[VMEM] * len(operands) + [ANY] * len(after),
        out_specs=tuple(VMEM for _ in out_shape),
        compiler_params=pltpu.CompilerParams(vmem_limit_bytes=limit * MIB),
        cost_estimate=pl.CostEstimate(flops=cost or 0, bytes_accessed=1024, transcendentals=0),
    )(*operands, *after)


def pack_kernel(sources, layout, *refs):
    for out_ref, spans in zip(refs[len(refs) - len(layout) :], layout):
        at = 0
        for source, start, count in spans:
            out_ref[at : at + count] = refs[source][start : start + count]
            at += count


def pack(sources, layout, after):
    columns, dtype = sources[0].shape[1], sources[0].dtype
    shapes = tuple(jax.ShapeDtypeStruct((sum(span[2] for span in spans), columns), dtype) for spans in layout)
    return local_call(functools.partial(pack_kernel, len(sources), layout), shapes, sources, after, 6)


class Gather:
    def __init__(self, block, rows):
        self.block, self.rows = block, rows
        self.height = block.shape[0]
        self.half = self.height // 2
        self.pieces = []
        self.split = rows == 16
        if self.split:
            self.far, self.near, self.side = (swap(block, rows, mask) for mask in (8, 4, 2))
        else:
            self.pieces.append((lax.all_gather(block, "rows", axis=0, tiled=True), None))

    def add(self, array, parts):
        self.pieces.append((array, parts))
        self.pieces.append((swap(array, self.rows, 1), [(mask + 1, start, count) for mask, start, count in parts]))

    def second(self, after):
        height, half = self.height, self.half
        self.for_near, self.for_side = pack(
            [self.far, self.near, self.side],
            [[(0, 0, height), (2, 0, half)], [(0, 0, height), (1, half, half)]],
            after,
        )
        self.by_near = swap(self.for_near, self.rows, 4)
        self.by_side = swap(self.for_side, self.rows, 2)

    def joining(self):
        return [self.block, self.far, self.near, self.side, self.by_near, self.by_side] if self.split else []

    def third(self, joined, other):
        height, half = self.height, self.half
        self.add(
            joined,
            [(mask, 0, height) for mask in (0, 8, 4, 2)]
            + [(12, 0, height), (6, 0, half), (10, 0, height), (6, half, half)],
        )
        self.last = swap(other, self.rows, 2, 4)

    def fourth(self):
        height = self.height
        (self.tail,) = pack([self.last], [[(0, 0, height)]], [])
        self.add(self.tail, [(14, 0, height)])


def product_kernel(parts, has_total, factor_ref, *refs):
    own_row, own_group = lax.axis_index("rows"), lax.axis_index("cols")
    groups, height, _ = factor_ref.shape
    send_ref, vector_ref = refs[-2:]
    for piece_ref, spans in zip(refs, parts):
        if spans is None:
            vector_ref[...] = piece_ref[...]
            continue
        at = 0
        for mask, start, count in spans:
            place = pl.multiple_of((own_row ^ mask) * height + start, count)
            vector_ref[pl.ds(place, count)] = piece_ref[at : at + count]
            at += count
    vector = vector_ref[...]
    for turn in range(groups - 1):
        group = lax.rem(own_group + 1 + turn, groups)
        span = pl.ds(turn * height, height)
        result = jnp.dot(factor_ref[group], vector, preferred_element_type=jnp.float32)
        if has_total:
            result = result + refs[len(parts)][span]
        send_ref[span] = result.astype(send_ref.dtype)


def own_kernel(has_total, factor_ref, vector_ref, *refs):
    groups, height, _ = factor_ref.shape
    result = jnp.dot(factor_ref[lax.axis_index("cols")], vector_ref[...], preferred_element_type=jnp.float32)
    refs[-1][...] = result + refs[0][pl.ds((groups - 1) * height, height)] if has_total else result


def total_kernel(has_total, factor_ref, vector_ref, *refs):
    own_group = lax.axis_index("cols")
    groups, height, _ = factor_ref.shape

    def one(turn, carry):
        group = lax.rem(own_group + 1 + turn, groups)
        span = pl.ds(pl.multiple_of(turn * height, height), height)
        result = jnp.dot(factor_ref[group], vector_ref[...], preferred_element_type=jnp.float32)
        refs[-1][span] = result + refs[0][span] if has_total else result
        return carry

    lax.fori_loop(0, groups, one, 0)


def product(factor, pieces, total, after):
    groups, height, width = factor.shape
    columns = pieces[0][0].shape[1]
    given = [] if total is None else [total]
    return local_call(
        functools.partial(product_kernel, [spans for _, spans in pieces], len(given)),
        (
            jax.ShapeDtypeStruct(((groups - 1) * height, columns), jnp.bfloat16),
            jax.ShapeDtypeStruct((width, columns), jnp.bfloat16),
        ),
        [factor, *(array for array, _ in pieces), *given],
        after,
        14,
    )


def own_product(factor, vector, total):
    given = [] if total is None else [total]
    _, height, width = factor.shape
    columns = vector.shape[1]
    return local_call(
        functools.partial(own_kernel, len(given)),
        (jax.ShapeDtypeStruct((height, columns), jnp.float32),),
        [factor, vector, *given],
        [],
        14,
        2 * height * width * columns,
    )[0]


def add_product(factor, vector, total):
    groups, height, width = factor.shape
    columns = vector.shape[1]
    given = [] if total is None else [total]
    return local_call(
        functools.partial(total_kernel, len(given)),
        (jax.ShapeDtypeStruct((groups * height, columns), jnp.float32),),
        [factor, vector, *given],
        [],
        14,
        2 * groups * height * width * columns,
    )[0]


def fold_kernel(shares, has_right, joins, keep_ref, *refs):
    total = keep_ref[...]
    for share_ref in refs[:shares]:
        total = total + share_ref[...].astype(jnp.float32)
    outs = list(refs[shares + has_right + joins :])
    if has_right:
        outs.pop(0)[...] = (refs[shares][...] - total).astype(jnp.bfloat16)
    else:
        outs.pop(0)[...] = total.astype(jnp.bfloat16)
        outs.pop(0)[...] = total
    if joins:
        joined_ref, other_ref = outs
        sources = refs[shares + has_right :][:joins]
        at = 0
        for source_ref in sources:
            count = source_ref.shape[0]
            joined_ref[at : at + count] = source_ref[...]
            at += count
        is_odd = lax.rem(lax.axis_index("rows"), 2) == 1
        height = other_ref.shape[0]
        other_ref[...] = jnp.where(is_odd, sources[5][:height], sources[4][:height])


def fold(keep, shares, right, joining):
    rounded = jax.ShapeDtypeStruct(keep.shape, jnp.bfloat16)
    given = [] if right is None else [right]
    out_shape = [rounded]
    if right is None:
        out_shape.append(jax.ShapeDtypeStruct(keep.shape, jnp.float32))
    if joining:
        rows, columns = sum(array.shape[0] for array in joining), keep.shape[1]
        out_shape.append(jax.ShapeDtypeStruct((rows, columns), jnp.bfloat16))
        out_shape.append(jax.ShapeDtypeStruct(keep.shape, jnp.bfloat16))
    kernel = functools.partial(fold_kernel, len(shares), len(given), len(joining))
    return list(local_call(kernel, tuple(out_shape), [keep, *shares, *given, *joining], [], 8))


def start_third(joining):
    height = joining[0].shape[0]
    is_odd = lax.rem(lax.axis_index("rows"), 2) == 1
    (joined,) = pack(joining, [[(i, 0, array.shape[0]) for i, array in enumerate(joining)]], [])
    return joined, jnp.where(is_odd, joining[5][:height], joining[4][:height])


def forward_solve(rows, cols, right_side, inverse_blocks, lower_blocks):
    panels, _, height, columns = right_side.shape
    chunks = 2 if rows == 16 and cols == 2 else 1
    width = columns // chunks
    steps = 2 * panels - 1
    solved = [[None] * chunks for _ in range(panels)]
    totals = [{} for _ in range(chunks)]
    factors = {}

    def right(current, chunk):
        return right_side[current, 0, :, chunk * width : (chunk + 1) * width]

    def load(step, after):
        current = step // 2
        blocks = inverse_blocks if step % 2 == 0 else lower_blocks
        if after is not None:
            blocks, _ = lax.optimization_barrier((blocks, after))
        if step % 2 == 0:
            loaded = {current: blocks[current]}
        else:
            loaded = {later: blocks[pair_index(later, current)] for later in range(current + 1, panels)}
        factors[step] = loaded
        return list(loaded.values())

    def multiply(step, chunk, gather, after):
        current, solving = step // 2, step % 2 == 0
        first = current if solving else current + 1
        total = None if solving else totals[chunk].pop(first, None)
        sends, vector = product(factors[step][first], gather.pieces, total, after)
        keep = own_product(factors[step][first], vector, total)
        made = []
        if not solving:
            for later in range(current + 2, panels):
                old = totals[chunk].get(later)
                totals[chunk][later] = add_product(factors[step][later], vector, old)
                made.append(totals[chunk][later])
        return sends, keep, made

    def finish(step, chunk, sends, keep, following):
        current, solving = step // 2, step % 2 == 0
        shares = []
        for turn in range(1, cols):
            share = sends[(turn - 1) * height : turn * height]
            shares.append(lax.ppermute(share, "cols", [(i, (i + turn) % cols) for i in range(cols)]))
        joining = following.joining() if following else []
        made = fold(keep, shares, None if solving else right(current + 1, chunk), joining)
        vectors[chunk] = made.pop(0)
        if solving:
            solved[current][chunk] = made.pop(0)
        if joining:
            following.third(*made)

    vectors = [right(0, chunk).astype(jnp.bfloat16) for chunk in range(chunks)]
    load(0, None)
    if chunks == 1:
        for step in range(steps):
            if step + 1 < steps:
                load(step + 1, vectors[0])
            sends, keep, _ = multiply(step, 0, Gather(vectors[0], rows), [])
            finish(step, 0, sends, keep, None)
    else:
        made = []
        gather = Gather(vectors[0], rows)
        gather.second([])
        gather.third(*start_third(gather.joining()))
        for step in range(steps):
            for chunk in range(chunks):
                other = 1 - chunk
                following = None
                gather.fourth()
                if step + chunk < steps:
                    following = Gather(vectors[other], rows)
                    loaded = load(step + 1, vectors[other]) if chunk == 0 and step + 1 < steps else []
                    following.second([gather.tail, *made, *loaded])
                sends, keep, made = multiply(step, chunk, gather, [following.for_near] if following else [])
                finish(step, chunk, sends, keep, following)
                gather = following
    return jnp.stack([jnp.concatenate(part, axis=1) for part in solved])[:, None]


def solution(mesh):
    return jax.shard_map(
        functools.partial(forward_solve, mesh.shape["rows"], mesh.shape["cols"]),
        mesh=mesh,
        in_specs=(
            P(None, "cols", "rows", None),
            P(None, None, "rows", "cols"),
            P(None, None, "rows", "cols"),
        ),
        out_specs=P(None, "cols", "rows", None),
        check_vma=False,
    )
```
